128 devices in a mesh: row: 4 (over x), col: 32 (over z, y, core).
Axes of the slice: x: 4, y: 4, z: 4, core: 2. Of those that a mesh axis runs over, the one named last changes fastest.
Arguments:
- tokens: bfloat16 [512, 8192], P('col', 'row'), may hold values from -6 to 6
- out_grad: bfloat16 [512, 8192], P('col', 'row'), may hold values from -6 to 6
- gate_weight: bfloat16 [8192, 29568], P('row', 'col'), may hold values from -0.0625 to 0.0625
- up_weight: bfloat16 [8192, 29568], P('row', 'col'), may hold values from -0.0625 to 0.0625
- down_weight: bfloat16 [29568, 8192], P('col', 'row'), may hold values from -0.03125 to 0.03125
Outputs:
- input_grad: bfloat16 [512, 8192], P('col', 'row')
- gate_wgrad: bfloat16 [8192, 29568], P('row', 'col')
- up_wgrad: bfloat16 [8192, 29568], P('row', 'col')
- down_wgrad: bfloat16 [29568, 8192], P('col', 'row')
The draws below stay inside these ranges and needn't reach their ends.
All inputs are finite; a program needn't handle non-finite values.
Results may differ from the reference program's by a relative error of at most 0.005.
Values may be sent and summed in bfloat16 or wider, within the bound.
No kernel may reach another device: no remote copies, remote signals or barrier semaphores. Data moves between devices by JAX's collectives and lax.ppermute only.
A program may use at most 128 MiB of HBM per device.

```python
import math
import jax
import jax.numpy as jnp
from jax import lax

D = 8192
FF = 29568
TOKENS = 512


def block_scale(stream_key, shape, shards, least, top_value):
    loudness = 1.0
    for axis_at, parts in shards:
        heights = jax.random.uniform(jax.random.fold_in(jax.random.fold_in(stream_key, 6), axis_at), (parts,), jnp.float32, least / len(shards), top_value / len(shards))
        loudness = loudness * jnp.repeat(jnp.exp(heights), shape[axis_at] // parts).reshape((-1,) + (1,) * (len(shape) - 1 - axis_at))
    return loudness


def bell_draw(own_key, dims, width, reach, shards=(), kind=jnp.bfloat16):
    values = width * jax.random.normal(own_key, dims, jnp.float32)
    if shards:
        values = values * block_scale(own_key, dims, shards, -0.22, 0.18)
    return jnp.clip(values, -reach, reach).astype(kind)


def setup_inputs(seed: int = 0) -> dict:
    splits = jax.random.split(jax.random.key(seed), 6)
    return {
        "tokens": bell_draw(splits[0], (TOKENS, D), 1.0, 6.0, ((0, 32), (1, 4))),
        "out_grad": bell_draw(splits[1], (TOKENS, D), 1.0, 6.0, ((0, 32), (1, 4))),
        "gate_weight": bell_draw(splits[2], (D, FF), D ** -0.5, 0.0625, ((0, 4), (1, 32))),
        "up_weight": bell_draw(splits[3], (D, FF), D ** -0.5, 0.0625, ((0, 4), (1, 32))),
        "down_weight": bell_draw(splits[4], (FF, D), FF ** -0.5, 0.03125, ((0, 32), (1, 4))),
    }


def contract(left, right, left_dim, right_dim):
    return lax.dot_general(left, right, (((left_dim,), (right_dim,)), ((), ())), preferred_element_type=jnp.float32)

def reference(tokens, out_grad, gate_weight, up_weight, down_weight):
    factor = 1.0 / math.sqrt(TOKENS)
    gate = jnp.dot(tokens, gate_weight, preferred_element_type=jnp.float32)
    upward = jnp.dot(tokens, up_weight, preferred_element_type=jnp.float32)
    hid_grad = contract(out_grad, down_weight, 1, 1)
    sig = jax.nn.sigmoid(gate)
    act = gate * sig
    hidden = (act * upward).astype(jnp.bfloat16)
    gate_grad = (hid_grad * upward * sig * (1.0 + gate * (1.0 - sig))).astype(jnp.bfloat16)
    up_grad = (hid_grad * act).astype(jnp.bfloat16)
    input_grad = (contract(gate_grad, gate_weight, 1, 1) + contract(up_grad, up_weight, 1, 1)).astype(jnp.bfloat16)
    gate_wgrad = (contract(tokens, gate_grad, 0, 0) * factor).astype(jnp.bfloat16)
    up_wgrad = (contract(tokens, up_grad, 0, 0) * factor).astype(jnp.bfloat16)
    down_wgrad = (contract(hidden, out_grad, 0, 0) * factor).astype(jnp.bfloat16)
    return (input_grad, gate_wgrad, up_wgrad, down_wgrad)
```

```python
import math

import jax
import jax.numpy as jnp
from jax import lax
from jax.sharding import PartitionSpec as P

BF16 = jnp.bfloat16
F32 = jnp.float32
ROWS, PLANES, LINES, CORES = 4, 4, 4, 2
CHUNKS = ((0,), (1,), (-1,), (2,))


def device(x, z, y, c):
    return ((x % ROWS) * PLANES + z % PLANES) * LINES * CORES + (y % LINES) * CORES + c


def route(target):
    return [
        (device(x, z, y, c), device(*target(x, z, y, c)))
        for x in range(ROWS)
        for z in range(PLANES)
        for y in range(LINES)
        for c in range(CORES)
    ]


def send(value, target):
    return lax.ppermute(value, ("row", "col"), route(target))


def way(c):
    return 1 - 2 * c


def slot_offset(x, c, slot):
    return x + (0, -way(c), way(c), 2)[slot]


def contract(left, right, left_dim, right_dim):
    return lax.dot_general(
        left, right, (((left_dim,), (right_dim,)), ((), ())), preferred_element_type=F32
    )


def swap_cores(value):
    return send(value, lambda x, z, y, c: (x, z, y, 1 - c))


def join_cores(mine, others):
    others = jnp.stack([others[0], others[2], others[1], others[3]])
    return jnp.stack([mine, others], axis=1)


def swiglu_backward(gate, upward, hid_grad):
    sig = jax.nn.sigmoid(gate)
    act = gate * sig
    hidden = (act * upward).astype(BF16)
    gate_grad = (hid_grad * upward * sig * (1.0 + gate * (1.0 - sig))).astype(BF16)
    up_grad = (hid_grad * act).astype(BF16)
    return (hidden, gate_grad, up_grad)


def forward(x, z, y, c):
    return (x + way(c), z, y, c)


def backward(x, z, y, c):
    return (x - way(c), z, y, c)


def local(tokens, out_grad, gate_weight, up_weight, down_weight):
    width = gate_weight.shape[1]
    factor = 1.0 / math.sqrt(tokens.shape[0] * 32)
    block = jnp.stack([tokens, out_grad])
    line = jnp.stack(
        [
            send(block, lambda x, z, y, c, s=s: (x, z, y - slot_offset(x, c, s), c))
            for s in range(4)
        ]
    )
    planes = {0: line}
    for dz in (1, -1, 2):
        planes[dz] = send(line, lambda x, z, y, c: (x, z - dz, y, c))

    def joined(dzs):
        parts = [join_cores(planes[dz], swap_cores(planes[dz])) for dz in dzs]
        both = jnp.stack(parts, axis=1)
        both = jnp.moveaxis(both, 3, 0)
        return both.reshape(2, -1, both.shape[-1])

    all_x, all_g, all_q = [], [], []
    slots = []
    for dzs in CHUNKS:
        x_rows, g_rows = joined(dzs)
        part = jnp.concatenate(
            [
                jnp.dot(x_rows, gate_weight, preferred_element_type=F32),
                jnp.dot(x_rows, up_weight, preferred_element_type=F32),
                contract(g_rows, down_weight, 1, 1),
            ],
            axis=1,
        ).reshape(4, -1, 3 * width)
        far = send(part[3].astype(BF16), forward)
        near = send(part[1].astype(BF16), backward)
        relay = send((part[2] + far.astype(F32)).astype(BF16), forward)
        whole = part[0] + near.astype(F32) + relay.astype(F32)
        mine = jnp.concatenate(
            swiglu_backward(whole[:, :width], whole[:, width : 2 * width], whole[:, 2 * width :]),
            axis=1,
        )
        behind = send(mine, forward)
        ahead = send(mine, backward)
        across = send(behind, forward)
        q = jnp.concatenate([mine, behind, ahead, across])
        all_x.append(x_rows)
        all_g.append(g_rows)
        all_q.append(q)
        grad = contract(q[:, width : 2 * width], gate_weight, 1, 1) + contract(
            q[:, 2 * width :], up_weight, 1, 1
        )
        grad = grad.reshape(4, len(dzs), 2, 16, -1)
        away = grad[:, :, 1]
        away = jnp.stack([away[0], away[2], away[1], away[3]])
        here = grad[:, :, 0] + swap_cores(away)
        for i, dz in enumerate(dzs):
            if dz == 0:
                slots.append(here[:, i])
            else:
                there = send(here[:, i].astype(BF16), lambda x, z, y, c: (x, z + dz, y, c))
                slots.append(there.astype(F32))
    total = sum(slots)
    input_grad = sum(
        send(total[s].astype(BF16), lambda x, z, y, c, s=s: (x, z, y + slot_offset(x, c, s), c)).astype(F32)
        for s in range(4)
    ).astype(BF16)
    x_all, g_all, q_all = (jnp.concatenate(v) for v in (all_x, all_g, all_q))
    gate_wgrad = (contract(x_all, q_all[:, width : 2 * width], 0, 0) * factor).astype(BF16)
    up_wgrad = (contract(x_all, q_all[:, 2 * width :], 0, 0) * factor).astype(BF16)
    down_wgrad = (contract(q_all[:, :width], g_all, 0, 0) * factor).astype(BF16)
    return (input_grad, gate_wgrad, up_wgrad, down_wgrad)


def solution(mesh):
    placed = (P("col", "row"), P("col", "row"), P("row", "col"), P("row", "col"), P("col", "row"))
    return jax.shard_map(
        local,
        mesh=mesh,
        in_specs=placed,
        out_specs=(P("col", "row"), P("row", "col"), P("row", "col"), P("col", "row")),
        check_vma=False,
    )
```

```python
import functools
import math

import jax
import jax.numpy as jnp
from jax import lax
from jax.experimental import pallas as pl
from jax.experimental.pallas import tpu as pltpu
from jax.sharding import PartitionSpec as P

BF16 = jnp.bfloat16
F32 = jnp.float32
ROWS, PLANES, LINES, CORES = 4, 4, 4, 2
FLIP = (0, 2, 1, 3)
MAIN, TAIL, STEP, LANES = 896, 28, 32, 128
PACKED = 3 * MAIN + LANES
TILES = ((0, 256), (256, 256), (512, 256), (768, 128))
VMEM = pl.BlockSpec(memory_space=pltpu.VMEM)
SMEM = pl.BlockSpec(memory_space=pltpu.SMEM)


def device(x, z, y, c):
    return ((x % ROWS) * PLANES + z % PLANES) * LINES * CORES + (y % LINES) * CORES + c


def send(value, target):
    pairs = [
        (device(x, z, y, c), device(*target(x, z, y, c, 1 - 2 * c)))
        for x in range(ROWS)
        for z in range(PLANES)
        for y in range(LINES)
        for c in range(CORES)
    ]
    return lax.ppermute(value, ("row", "col"), pairs)


def swap_cores(value):
    return send(value, lambda x, z, y, c, w: (x, z, y, 1 - c))


def flip(value):
    return jnp.stack([value[i] for i in FLIP])


def after(value, *others):
    return lax.optimization_barrier((value, others))[0]


def call(kernel, outs, specs, scratch, cost, name):
    return pl.pallas_call(
        kernel,
        out_shape=[jax.ShapeDtypeStruct(s, t) for s, t in outs],
        in_specs=specs,
        out_specs=[VMEM] * len(outs),
        scratch_shapes=scratch,
        compiler_params=pltpu.CompilerParams(vmem_limit_bytes=40 * 2**20),
        cost_estimate=pl.CostEstimate(flops=cost[0], bytes_accessed=cost[1], transcendentals=0),
        name=name,
    )


def dot(left, right, dims):
    return lax.dot_general(left, right, (dims, ((), ())), preferred_element_type=F32)


def forward_kernel(layout, count, at, gate_w, up_w, down_w, tail_x, tail_g, *refs):
    sources, refs = refs[: layout[0]], refs[layout[0] :]
    x_ref, g_ref, far, near, relay, own, part = refs
    for row, (source, index) in enumerate(layout[1]):
        x_ref[row * 16 : row * 16 + 16] = sources[source][(*index, 0)]
        g_ref[row * 16 : row * 16 + 16] = sources[source][(*index, 1)]
    tails = dot(x_ref[...], tail_x[...], ((1,), (1,))) + dot(g_ref[...], tail_g[...], ((1,), (1,)))
    part[:, :, 3 * MAIN :] = tails.reshape(4, count, LANES)
    for i in range(3):
        rows, weight = (x_ref, x_ref, g_ref)[i], (gate_w, up_w, down_w)[i]
        for start, size in TILES:
            product = dot(weight[start : start + size], rows[...], ((1,), (1,))).T
            part[:, :, i * MAIN + start : i * MAIN + start + size] = product.reshape(4, count, size)
    own[...] = part[at[0]]
    near[...] = part[at[1]].astype(BF16)
    relay[...] = part[at[2]]
    far[...] = part[at[3]].astype(BF16)


def forward(at, weights, tails, sources, layout):
    rows = len(layout) * 16
    count, depth = rows // 4, tails[0].shape[1]
    kernel = functools.partial(forward_kernel, (len(sources), layout), count)
    return call(
        kernel,
        [((rows, depth), BF16)] * 2
        + [((count, PACKED), BF16)] * 2
        + [((count, PACKED), F32)] * 2,
        [SMEM] + [VMEM] * (5 + len(sources)),
        [pltpu.VMEM((4, count, PACKED), F32)],
        (6 * rows * depth * (MAIN + TAIL), 6 * MAIN * depth),
        "forward_products",
    )(at, *weights, tails[0], tails[1], *sources)


def swiglu_backward(gate, upward, hid_grad):
    sig = 1.0 / (1.0 + jnp.exp(-gate))
    act = gate * sig
    return (
        act * upward,
        hid_grad * upward * sig * (1.0 + gate * (1.0 - sig)),
        hid_grad * act,
    )


def activation_kernel(own, near, relay, mine):
    def whole(start, size):
        cut = slice(start, start + size)
        return own[:, cut] + near[:, cut].astype(F32) + relay[:, cut].astype(F32)

    for start in range(0, MAIN, LANES):
        parts = swiglu_backward(*(whole(i * MAIN + start, LANES) for i in range(3)))
        for i, v in enumerate(parts):
            mine[:, i * MAIN + start : i * MAIN + start + LANES] = v.astype(BF16)
    gate = whole(3 * MAIN, LANES)
    hidden, gate_grad, up_grad = swiglu_backward(
        gate, pltpu.roll(gate, LANES - STEP, 1), pltpu.roll(gate, LANES - 2 * STEP, 1)
    )
    lane = lax.broadcasted_iota(jnp.int32, gate.shape, 1)
    tail = jnp.where(lane < 2 * STEP, pltpu.roll(gate_grad, STEP, 1), pltpu.roll(up_grad, 2 * STEP, 1))
    tail = jnp.where(lane < STEP, hidden, tail)
    mine[:, 3 * MAIN :] = jnp.where(lane < 3 * STEP, tail, 0.0).astype(BF16)


def activation(own, near, relay):
    return call(
        activation_kernel,
        [(near.shape, BF16)],
        [VMEM] * 3,
        [],
        (20 * own.size, 10 * own.size),
        "activation",
    )(own, near, relay)[0]


def input_kernel(planes, at, gate_w, up_w, tail, mine, behind, ahead, across, q, keep, away):
    count = mine.shape[0]
    for i, v in enumerate((mine, behind, ahead, across)):
        q[at[i]] = v[...]
    def rows(start, size):
        return q[:, :, start : start + size].reshape(4 * count, size)

    for start in range(0, tail.shape[1], 512):
        cut = slice(start, start + 512)
        grad = (
            dot(rows(MAIN, MAIN), gate_w[:MAIN, cut], ((1,), (0,)))
            + dot(rows(2 * MAIN, MAIN), up_w[:MAIN, cut], ((1,), (0,)))
            + dot(rows(3 * MAIN, LANES), tail[:, cut], ((1,), (0,)))
        )
        for line in range(4):
            first = line * count
            if planes == 1:
                keep[line, :, cut] = grad[first : first + 16]
                away[FLIP[line], :, cut] = grad[first + 16 : first + 32]
            else:
                keep[line, 0, :, cut] = grad[first : first + 16]
                keep[line, 1, :, cut] = grad[first + 16 : first + 32]
                away[FLIP[line], 1, :, cut] = grad[first + 32 : first + 48]
                away[FLIP[line], 0, :, cut] = grad[first + 48 : first + 64]


def input_gradient(at, weights, tail, pieces):
    count, depth = pieces[0].shape[0], tail.shape[1]
    planes = count // 32
    part = (4, 16, depth) if planes == 1 else (4, 2, 16, depth)
    return call(
        functools.partial(input_kernel, planes),
        [((4, count, PACKED), BF16), (part, F32), (part, F32)],
        [SMEM] + [VMEM] * 7,
        [],
        (16 * count * depth * (MAIN + TAIL), 4 * MAIN * depth),
        "input_products",
    )(at, weights[0], weights[1], tail, *pieces)


def weight_kernel(factor, x, g, *refs):
    chunks, (gate_out, up_out, down_out, turned) = refs[:-4], refs[-4:]

    @pl.when(pl.program_id(0) == 0)
    def _():
        first = 0
        for q in chunks:
            rows = q.shape[0]
            for start in range(0, PACKED, LANES):
                turned[start : start + LANES, first : first + rows] = q[:, start : start + LANES].T
            first += rows

    x_tail = dot(turned[3 * MAIN :], x[...], ((1,), (0,))) * factor
    g_tail = dot(turned[3 * MAIN :], g[...], ((1,), (0,))) * factor
    for i, (out, rows, tail) in enumerate(((down_out, g, g_tail), (gate_out, x, x_tail), (up_out, x, x_tail))):
        product = dot(turned[i * MAIN : (i + 1) * MAIN], rows[...], ((1,), (0,))) * factor
        out[:MAIN] = product.astype(BF16)
        out[MAIN:] = tail[i * STEP : i * STEP + TAIL].astype(BF16)


def weight_gradients(x, g, chunks, factor):
    tokens, depth = x.shape
    width = 256
    column = pl.BlockSpec((tokens, width), lambda i: (0, i))
    out = pl.BlockSpec((MAIN + TAIL, width), lambda i: (0, i))
    return pl.pallas_call(
        functools.partial(weight_kernel, factor),
        grid=(depth // width,),
        out_shape=[jax.ShapeDtypeStruct((MAIN + TAIL, depth), BF16)] * 3,
        in_specs=[column, column] + [pl.BlockSpec(q.shape, lambda i: (0, 0)) for q in chunks],
        out_specs=[out] * 3,
        scratch_shapes=[pltpu.VMEM((PACKED, tokens), BF16)],
        compiler_params=pltpu.CompilerParams(vmem_limit_bytes=40 * 2**20),
        cost_estimate=pl.CostEstimate(
            flops=6 * tokens * depth * (MAIN + TAIL), bytes_accessed=6 * MAIN * depth, transcendentals=0
        ),
        name="weight_products",
    )(x, g, *chunks)


def x_along(x, z, y, c, w):
    return (x + w, z, y, c)


def x_against(x, z, y, c, w):
    return (x - w, z, y, c)


def gather(tokens, out_grad):
    block = jnp.stack([tokens, out_grad])
    pair = jnp.stack([block, swap_cores(block)])
    line_across = send(block, lambda x, z, y, c, w: (x, z, y + 2, c))
    line_prev = send(pair, lambda x, z, y, c, w: (x, z, y + w, c))
    other = swap_cores(jnp.concatenate([line_prev, line_across[None]]))
    own = jnp.stack([pair, line_prev, other[1::-1], jnp.stack([line_across, other[2]])])
    prev = send(own, lambda x, z, y, c, w: (x, z + w, y, c))
    lines, cores = range(4), range(2)
    yield (own,), [(0, (l, c)) for l in lines for c in cores]
    last = yield prev
    half = after(own[:, 0], prev)
    following = swap_cores(prev)
    half = send(half, lambda x, z, y, c, w: (x, z + 2, y, c))
    last = yield (
        (prev, following),
        [b for l in lines for b in [(0, (l, 0)), (0, (l, 1)), (1, (FLIP[l], 1)), (1, (FLIP[l], 0))]],
    )
    other_half = swap_cores(after(half, last))
    yield (half, other_half), [b for l in lines for b in [(0, (l,)), (1, (FLIP[l],))]]


def local(tokens, out_grad, gate_weight, up_weight, down_weight):
    depth = tokens.shape[1]
    factor = 1.0 / math.sqrt(tokens.shape[0] * PLANES * LINES * CORES)
    me = lax.axis_index("row")
    way = 1 - 2 * lax.rem(lax.axis_index("col"), CORES)
    at = jnp.stack([lax.rem(me + off + 4, 4) for off in (0, -way, way, 2)])
    weights = (gate_weight.T, up_weight.T, down_weight)
    ends = [jnp.pad(w[MAIN:], ((0, STEP - TAIL), (0, 0))) for w in weights]
    none = jnp.zeros_like(ends[0])
    tails = (
        jnp.concatenate([ends[0], ends[1], none, none]),
        jnp.concatenate([none, none, ends[2], none]),
        jnp.concatenate([none, ends[0], ends[1], none]),
    )

    chunks = gather(tokens, out_grad)
    last = None
    state = [{} for _ in range(3)]

    for i, s in enumerate(state):
        sources, layout = chunks.send(last)
        if last is not None:
            sources = after(sources, last)
        s["x"], s["g"], far, near, relay, own = forward(at, weights, tails, sources, layout)
        near = send(near, x_against)
        relay = (relay + send(far, x_along).astype(F32)).astype(BF16)
        if i == 0:
            prev = next(chunks)
            own = after(own, prev)
        mine = activation(own, near, send(relay, x_along))
        behind = send(mine, x_along)
        ahead = send(mine, x_against)
        pieces = (mine, behind, ahead, send(behind, x_along))
        q, keep, away = input_gradient(at, weights, tails[2], pieces)
        s["q"] = q.reshape(-1, PACKED)
        s["here"] = keep, swap_cores(away)
        if i == 0:
            last = mine
            first = (behind, ahead)
        else:
            last = first

    total = sum(state[0]["here"])
    here = sum(state[1]["here"])
    got = send(here.astype(BF16), lambda x, z, y, c, w: (x, z - w, y, c))
    here = sum(state[2]["here"])
    total += send(here.astype(BF16), lambda x, z, y, c, w: (x, z + 2, y, c)).astype(F32)
    all_x, all_g, all_q = ([s[k] for s in state] for k in ("x", "g", "q"))
    gate_wgrad, up_wgrad, down_wgrad = weight_gradients(
        after(jnp.concatenate(all_x), here), jnp.concatenate(all_g), all_q, factor
    )
    got = after(got, down_wgrad)
    rest = swap_cores(flip(got[:, 1]))
    total += got[:, 0].astype(F32) + rest.astype(F32)
    sent = total.astype(BF16)
    input_grad = (
        total[0]
        + send(sent[1], lambda x, z, y, c, w: (x, z, y - w, c)).astype(F32)
        + send(sent[2], lambda x, z, y, c, w: (x, z, y + w, c)).astype(F32)
        + send(sent[3], lambda x, z, y, c, w: (x, z, y + 2, c)).astype(F32)
    ).astype(BF16)
    return (input_grad, gate_wgrad.T, up_wgrad.T, down_wgrad)


def solution(mesh):
    placed = (P("col", "row"), P("col", "row"), P("row", "col"), P("row", "col"), P("col", "row"))
    return jax.shard_map(
        local,
        mesh=mesh,
        in_specs=placed,
        out_specs=(P("col", "row"), P("row", "col"), P("row", "col"), P("col", "row")),
        check_vma=False,
    )
```

```python
import functools
import math

import jax
import jax.numpy as jnp
from jax import lax
from jax.experimental import pallas as pl
from jax.experimental.pallas import tpu as pltpu
from jax.sharding import PartitionSpec as P

BF16 = jnp.bfloat16
F32 = jnp.float32
ROWS, PLANES, LINES, CORES = 4, 4, 4, 2
FLIP = (0, 2, 1, 3)
MAIN, TAIL, STEP, LANES = 896, 28, 32, 128
PACKED = 3 * MAIN + LANES
TILES = ((0, MAIN),)
VMEM = pl.BlockSpec(memory_space=pltpu.VMEM)
SMEM = pl.BlockSpec(memory_space=pltpu.SMEM)


def device(x, z, y, c):
    return ((x % ROWS) * PLANES + z % PLANES) * LINES * CORES + (y % LINES) * CORES + c


def send(value, target):
    pairs = [
        (device(x, z, y, c), device(*target(x, z, y, c, 1 - 2 * c)))
        for x in range(ROWS)
        for z in range(PLANES)
        for y in range(LINES)
        for c in range(CORES)
    ]
    return lax.ppermute(value, ("row", "col"), pairs)


def swap_cores(value):
    return send(value, lambda x, z, y, c, w: (x, z, y, 1 - c))


def flip(value):
    return jnp.stack([value[i] for i in FLIP])


def after(value, *others):
    return lax.optimization_barrier((value, others))[0]


def call(kernel, outs, specs, scratch, cost, name):
    return pl.pallas_call(
        kernel,
        out_shape=[jax.ShapeDtypeStruct(s, t) for s, t in outs],
        in_specs=specs,
        out_specs=[VMEM] * len(outs),
        scratch_shapes=scratch,
        compiler_params=pltpu.CompilerParams(vmem_limit_bytes=40 * 2**20),
        cost_estimate=pl.CostEstimate(flops=cost[0], bytes_accessed=cost[1], transcendentals=0),
        name=name,
    )


def dot(left, right, dims):
    return lax.dot_general(left, right, (dims, ((), ())), preferred_element_type=F32)


def forward_kernel(layout, count, at, gate_w, up_w, down_w, tail_x, tail_g, *refs):
    sources, refs = refs[: layout[0]], refs[layout[0] :]
    x_ref, g_ref, far, near, relay, own, part = refs
    for row, (source, index) in enumerate(layout[1]):
        x_ref[row * 16 : row * 16 + 16] = sources[source][(*index, 0)]
        g_ref[row * 16 : row * 16 + 16] = sources[source][(*index, 1)]
    tails = dot(x_ref[...], tail_x[...], ((1,), (1,))) + dot(g_ref[...], tail_g[...], ((1,), (1,)))
    part[:, :, 3 * MAIN :] = tails.reshape(4, count, LANES)
    for i in range(3):
        rows, weight = (x_ref, x_ref, g_ref)[i], (gate_w, up_w, down_w)[i]
        for start, size in TILES:
            product = dot(weight[start : start + size], rows[...], ((1,), (1,))).T
            part[:, :, i * MAIN + start : i * MAIN + start + size] = product.reshape(4, count, size)
    own[...] = part[at[0]]
    near[...] = part[at[1]].astype(BF16)
    relay[...] = part[at[2]]
    far[...] = part[at[3]].astype(BF16)


def forward(at, weights, tails, sources, layout):
    rows = len(layout) * 16
    count, depth = rows // 4, tails[0].shape[1]
    kernel = functools.partial(forward_kernel, (len(sources), layout), count)
    return call(
        kernel,
        [((rows, depth), BF16)] * 2
        + [((count, PACKED), BF16)] * 2
        + [((count, PACKED), F32)] * 2,
        [SMEM] + [VMEM] * (5 + len(sources)),
        [pltpu.VMEM((4, count, PACKED), F32)],
        (6 * rows * depth * (MAIN + TAIL), 6 * MAIN * depth),
        "forward_products",
    )(at, *weights, tails[0], tails[1], *sources)


def swiglu_backward(gate, upward, hid_grad):
    sig = 1.0 / (1.0 + jnp.exp(-gate))
    act = gate * sig
    return (
        act * upward,
        hid_grad * upward * sig * (1.0 + gate * (1.0 - sig)),
        hid_grad * act,
    )


def activation_kernel(own, near, relay, mine):
    def whole(start, size):
        cut = slice(start, start + size)
        return own[:, cut] + near[:, cut].astype(F32) + relay[:, cut].astype(F32)

    for start in range(0, MAIN, LANES):
        parts = swiglu_backward(*(whole(i * MAIN + start, LANES) for i in range(3)))
        for i, v in enumerate(parts):
            mine[:, i * MAIN + start : i * MAIN + start + LANES] = v.astype(BF16)
    gate = whole(3 * MAIN, LANES)
    hidden, gate_grad, up_grad = swiglu_backward(
        gate, pltpu.roll(gate, LANES - STEP, 1), pltpu.roll(gate, LANES - 2 * STEP, 1)
    )
    lane = lax.broadcasted_iota(jnp.int32, gate.shape, 1)
    tail = jnp.where(lane < 2 * STEP, pltpu.roll(gate_grad, STEP, 1), pltpu.roll(up_grad, 2 * STEP, 1))
    tail = jnp.where(lane < STEP, hidden, tail)
    mine[:, 3 * MAIN :] = jnp.where(lane < 3 * STEP, tail, 0.0).astype(BF16)


def activation(own, near, relay):
    return call(
        activation_kernel,
        [(near.shape, BF16)],
        [VMEM] * 3,
        [],
        (20 * own.size, 10 * own.size),
        "activation",
    )(own, near, relay)[0]


def input_kernel(planes, at, gate_w, up_w, tail, mine, behind, ahead, across, q, keep, away):
    count = mine.shape[0]
    for i, v in enumerate((mine, behind, ahead, across)):
        q[at[i]] = v[...]
    def rows(start, size):
        return q[:, :, start : start + size].reshape(4 * count, size)

    for start in range(0, tail.shape[1], 512):
        cut = slice(start, start + 512)
        grad = (
            dot(rows(MAIN, MAIN), gate_w[:MAIN, cut], ((1,), (0,)))
            + dot(rows(2 * MAIN, MAIN), up_w[:MAIN, cut], ((1,), (0,)))
            + dot(rows(3 * MAIN, LANES), tail[:, cut], ((1,), (0,)))
        )
        for line in range(4):
            first = line * count
            if planes == 1:
                keep[line, :, cut] = grad[first : first + 16]
                away[FLIP[line], :, cut] = grad[first + 16 : first + 32]
            else:
                keep[line, 0, :, cut] = grad[first : first + 16]
                keep[line, 1, :, cut] = grad[first + 16 : first + 32]
                away[FLIP[line], 1, :, cut] = grad[first + 32 : first + 48]
                away[FLIP[line], 0, :, cut] = grad[first + 48 : first + 64]


def input_gradient(at, weights, tail, pieces):
    count, depth = pieces[0].shape[0], tail.shape[1]
    planes = count // 32
    part = (4, 16, depth) if planes == 1 else (4, 2, 16, depth)
    return call(
        functools.partial(input_kernel, planes),
        [((4, count, PACKED), BF16), (part, F32), (part, F32)],
        [SMEM] + [VMEM] * 7,
        [],
        (16 * count * depth * (MAIN + TAIL), 4 * MAIN * depth),
        "input_products",
    )(at, weights[0], weights[1], tail, *pieces)


def weight_kernel(factor, x, g, *refs):
    chunks, (gate_out, up_out, down_out, turned) = refs[:-4], refs[-4:]

    @pl.when(pl.program_id(0) == 0)
    def _():
        first = 0
        for q in chunks:
            rows = q.shape[0]
            for start in range(0, PACKED, LANES):
                turned[start : start + LANES, first : first + rows] = q[:, start : start + LANES].T
            first += rows

    x_tail = dot(turned[3 * MAIN :], x[...], ((1,), (0,))) * factor
    g_tail = dot(turned[3 * MAIN :], g[...], ((1,), (0,))) * factor
    for i, (out, rows, tail) in enumerate(((down_out, g, g_tail), (gate_out, x, x_tail), (up_out, x, x_tail))):
        product = dot(turned[i * MAIN : (i + 1) * MAIN], rows[...], ((1,), (0,))) * factor
        out[:MAIN] = product.astype(BF16)
        out[MAIN:] = tail[i * STEP : i * STEP + TAIL].astype(BF16)


def weight_gradients(x, g, chunks, factor):
    tokens, depth = x.shape
    width = 512
    column = pl.BlockSpec((tokens, width), lambda i: (0, i))
    out = pl.BlockSpec((MAIN + TAIL, width), lambda i: (0, i))
    return pl.pallas_call(
        functools.partial(weight_kernel, factor),
        grid=(depth // width,),
        out_shape=[jax.ShapeDtypeStruct((MAIN + TAIL, depth), BF16)] * 3,
        in_specs=[column, column] + [pl.BlockSpec(q.shape, lambda i: (0, 0)) for q in chunks],
        out_specs=[out] * 3,
        scratch_shapes=[pltpu.VMEM((PACKED, tokens), BF16)],
        compiler_params=pltpu.CompilerParams(vmem_limit_bytes=40 * 2**20),
        cost_estimate=pl.CostEstimate(
            flops=6 * tokens * depth * (MAIN + TAIL), bytes_accessed=6 * MAIN * depth, transcendentals=0
        ),
        name="weight_products",
    )(x, g, *chunks)


def x_along(x, z, y, c, w):
    return (x + w, z, y, c)


def x_against(x, z, y, c, w):
    return (x - w, z, y, c)


def gather(tokens, out_grad):
    block = jnp.stack([tokens, out_grad])
    pair = jnp.stack([block, swap_cores(block)])
    line_across = send(block, lambda x, z, y, c, w: (x, z, y + 2, c))
    line_prev = send(pair, lambda x, z, y, c, w: (x, z, y + w, c))
    other = swap_cores(jnp.concatenate([line_prev, line_across[None]]))
    own = jnp.stack([pair, line_prev, other[1::-1], jnp.stack([line_across, other[2]])])
    prev = send(own, lambda x, z, y, c, w: (x, z + w, y, c))
    lines, cores = range(4), range(2)
    yield (own,), [(0, (l, c)) for l in lines for c in cores]
    last = yield prev
    half = after(own[:, 0], prev)
    following = swap_cores(prev)
    half = send(half, lambda x, z, y, c, w: (x, z + 2, y, c))
    last = yield (
        (prev, following),
        [b for l in lines for b in [(0, (l, 0)), (0, (l, 1)), (1, (FLIP[l], 1)), (1, (FLIP[l], 0))]],
    )
    other_half = swap_cores(after(half, last))
    yield (half, other_half), [b for l in lines for b in [(0, (l,)), (1, (FLIP[l],))]]


def local(tokens, out_grad, gate_weight, up_weight, down_weight):
    depth = tokens.shape[1]
    factor = 1.0 / math.sqrt(tokens.shape[0] * PLANES * LINES * CORES)
    me = lax.axis_index("row")
    way = 1 - 2 * lax.rem(lax.axis_index("col"), CORES)
    at = jnp.stack([lax.rem(me + off + 4, 4) for off in (0, -way, way, 2)])
    weights = (gate_weight.T, up_weight.T, down_weight)
    ends = [jnp.pad(w[MAIN:], ((0, STEP - TAIL), (0, 0))) for w in weights]
    none = jnp.zeros_like(ends[0])
    tails = (
        jnp.concatenate([ends[0], ends[1], none, none]),
        jnp.concatenate([none, none, ends[2], none]),
        jnp.concatenate([none, ends[0], ends[1], none]),
    )

    chunks = gather(tokens, out_grad)
    last = None
    state = [{} for _ in range(3)]

    for i, s in enumerate(state):
        sources, layout = chunks.send(last)
        if last is not None:
            sources = after(sources, last)
        s["x"], s["g"], far, near, relay, own = forward(at, weights, tails, sources, layout)
        near = send(near, x_against)
        relay = (relay + send(far, x_along).astype(F32)).astype(BF16)
        if i == 0:
            prev = next(chunks)
            own = after(own, prev)
        mine = activation(own, near, send(relay, x_along))
        behind = send(mine, x_along)
        ahead = send(mine, x_against)
        pieces = (mine, behind, ahead, send(behind, x_along))
        q, keep, away = input_gradient(at, weights, tails[2], pieces)
        s["q"] = q.reshape(-1, PACKED)
        s["here"] = keep, swap_cores(away)
        if i == 0:
            last = mine
        else:
            last = far

    total = sum(state[0]["here"])
    here = sum(state[1]["here"])
    got = send(here.astype(BF16), lambda x, z, y, c, w: (x, z - w, y, c))
    here = sum(state[2]["here"])
    total += send(here.astype(BF16), lambda x, z, y, c, w: (x, z + 2, y, c)).astype(F32)
    all_x, all_g, all_q = ([s[k] for s in state] for k in ("x", "g", "q"))
    gate_wgrad, up_wgrad, down_wgrad = weight_gradients(
        after(jnp.concatenate(all_x), here), jnp.concatenate(all_g), all_q, factor
    )
    got = after(got, down_wgrad)
    rest = swap_cores(flip(got[:, 1]))
    total += got[:, 0].astype(F32) + rest.astype(F32)
    sent = total.astype(BF16)
    input_grad = (
        total[0]
        + send(sent[1], lambda x, z, y, c, w: (x, z, y - w, c)).astype(F32)
        + send(sent[2], lambda x, z, y, c, w: (x, z, y + w, c)).astype(F32)
        + send(sent[3], lambda x, z, y, c, w: (x, z, y + 2, c)).astype(F32)
    ).astype(BF16)
    return (input_grad, gate_wgrad.T, up_wgrad.T, down_wgrad)


def solution(mesh):
    placed = (P("col", "row"), P("col", "row"), P("row", "col"), P("row", "col"), P("col", "row"))
    return jax.shard_map(
        local,
        mesh=mesh,
        in_specs=placed,
        out_specs=(P("col", "row"), P("row", "col"), P("row", "col"), P("col", "row")),
        check_vma=False,
    )
```

```python
import functools
import math

import jax
import jax.numpy as jnp
from jax import lax
from jax.experimental import pallas as pl
from jax.experimental.pallas import tpu as pltpu
from jax.sharding import PartitionSpec as P

BF16 = jnp.bfloat16
F32 = jnp.float32
ROWS, PLANES, LINES, CORES = 4, 4, 4, 2
FLIP = (0, 2, 1, 3)
MAIN, TAIL, STEP, LANES = 896, 28, 32, 128
PACKED = 3 * MAIN + LANES
TILES = ((0, MAIN),)
VMEM = pl.BlockSpec(memory_space=pltpu.VMEM)
SMEM = pl.BlockSpec(memory_space=pltpu.SMEM)


def device(x, z, y, c):
    return ((x % ROWS) * PLANES + z % PLANES) * LINES * CORES + (y % LINES) * CORES + c


def send(value, target):
    pairs = [
        (device(x, z, y, c), device(*target(x, z, y, c, 1 - 2 * c)))
        for x in range(ROWS)
        for z in range(PLANES)
        for y in range(LINES)
        for c in range(CORES)
    ]
    return lax.ppermute(value, ("row", "col"), pairs)


def swap_cores(value):
    return send(value, lambda x, z, y, c, w: (x, z, y, 1 - c))


def flip(value):
    return jnp.stack([value[i] for i in FLIP])


def after(value, *others):
    return lax.optimization_barrier((value, others))[0]


def call(kernel, outs, specs, scratch, cost, name):
    return pl.pallas_call(
        kernel,
        out_shape=[jax.ShapeDtypeStruct(s, t) for s, t in outs],
        in_specs=specs,
        out_specs=[VMEM] * len(outs),
        scratch_shapes=scratch,
        compiler_params=pltpu.CompilerParams(vmem_limit_bytes=40 * 2**20),
        cost_estimate=pl.CostEstimate(flops=cost[0], bytes_accessed=cost[1], transcendentals=0),
        name=name,
    )


def dot(left, right, dims):
    return lax.dot_general(left, right, (dims, ((), ())), preferred_element_type=F32)


def forward_kernel(layout, count, at, gate_w, up_w, down_w, *refs):
    sources, refs = refs[: layout[0]], refs[layout[0] :]
    x_ref, g_ref, far, near, relay, own, part, tail_x, tail_g = refs
    tail_x[...] = jnp.zeros_like(tail_x)
    tail_g[...] = jnp.zeros_like(tail_g)
    for i, (tail, w) in enumerate(((tail_x, gate_w), (tail_x, up_w), (tail_g, down_w))):
        tail[i * STEP : i * STEP + TAIL] = w[MAIN:]
    for row, (source, index) in enumerate(layout[1]):
        x_ref[row * 16 : row * 16 + 16] = sources[source][(*index, 0)]
        g_ref[row * 16 : row * 16 + 16] = sources[source][(*index, 1)]
    tails = dot(x_ref[...], tail_x[...], ((1,), (1,))) + dot(g_ref[...], tail_g[...], ((1,), (1,)))
    part[:, :, 3 * MAIN :] = tails.reshape(4, count, LANES)
    for i in range(3):
        rows, weight = (x_ref, x_ref, g_ref)[i], (gate_w, up_w, down_w)[i]
        for start, size in TILES:
            product = dot(weight[start : start + size], rows[...], ((1,), (1,))).T
            part[:, :, i * MAIN + start : i * MAIN + start + size] = product.reshape(4, count, size)
    own[...] = part[at[0]]
    near[...] = part[at[1]].astype(BF16)
    relay[...] = part[at[2]]
    far[...] = part[at[3]].astype(BF16)


def forward(at, weights, sources, layout):
    rows = len(layout) * 16
    count, depth = rows // 4, weights[2].shape[1]
    kernel = functools.partial(forward_kernel, (len(sources), layout), count)
    return call(
        kernel,
        [((rows, depth), BF16)] * 2
        + [((count, PACKED), BF16)] * 2
        + [((count, PACKED), F32)] * 2,
        [SMEM] + [VMEM] * (3 + len(sources)),
        [pltpu.VMEM((4, count, PACKED), F32)] + [pltpu.VMEM((LANES, depth), BF16)] * 2,
        (6 * rows * depth * (MAIN + TAIL), 6 * MAIN * depth),
        "forward_products",
    )(at, *weights, *sources)


def swiglu_backward(gate, upward, hid_grad):
    sig = 1.0 / (1.0 + jnp.exp(-gate))
    act = gate * sig
    return (
        act * upward,
        hid_grad * upward * sig * (1.0 + gate * (1.0 - sig)),
        hid_grad * act,
    )


def activation_kernel(own, near, relay, mine):
    def whole(start, size):
        cut = slice(start, start + size)
        return own[:, cut] + near[:, cut].astype(F32) + relay[:, cut].astype(F32)

    for start in range(0, MAIN, LANES):
        parts = swiglu_backward(*(whole(i * MAIN + start, LANES) for i in range(3)))
        for i, v in enumerate(parts):
            mine[:, i * MAIN + start : i * MAIN + start + LANES] = v.astype(BF16)
    gate = whole(3 * MAIN, LANES)
    hidden, gate_grad, up_grad = swiglu_backward(
        gate, pltpu.roll(gate, LANES - STEP, 1), pltpu.roll(gate, LANES - 2 * STEP, 1)
    )
    lane = lax.broadcasted_iota(jnp.int32, gate.shape, 1)
    tail = jnp.where(lane < 2 * STEP, pltpu.roll(gate_grad, STEP, 1), pltpu.roll(up_grad, 2 * STEP, 1))
    tail = jnp.where(lane < STEP, hidden, tail)
    mine[:, 3 * MAIN :] = jnp.where(lane < 3 * STEP, tail, 0.0).astype(BF16)


def activation(own, near, relay):
    return call(
        activation_kernel,
        [(near.shape, BF16)],
        [VMEM] * 3,
        [],
        (20 * own.size, 10 * own.size),
        "activation",
    )(own, near, relay)[0]


def input_kernel(planes, at, gate_w, up_w, tail, mine, behind, ahead, across, q, keep, away):
    count = mine.shape[0]
    for i, v in enumerate((mine, behind, ahead, across)):
        q[at[i]] = v[...]
    def rows(start, size):
        return q[:, :, start : start + size].reshape(4 * count, size)

    for start in range(0, tail.shape[1], 512):
        cut = slice(start, start + 512)
        grad = (
            dot(rows(MAIN, MAIN), gate_w[:MAIN, cut], ((1,), (0,)))
            + dot(rows(2 * MAIN, MAIN), up_w[:MAIN, cut], ((1,), (0,)))
            + dot(rows(3 * MAIN, LANES), tail[:, cut], ((1,), (0,)))
        )
        for line in range(4):
            first = line * count
            if planes == 1:
                keep[line, :, cut] = grad[first : first + 16]
                away[FLIP[line], :, cut] = grad[first + 16 : first + 32]
            else:
                keep[line, 0, :, cut] = grad[first : first + 16]
                keep[line, 1, :, cut] = grad[first + 16 : first + 32]
                away[FLIP[line], 1, :, cut] = grad[first + 32 : first + 48]
                away[FLIP[line], 0, :, cut] = grad[first + 48 : first + 64]


def input_gradient(at, weights, tail, pieces):
    count, depth = pieces[0].shape[0], tail.shape[1]
    planes = count // 32
    part = (4, 16, depth) if planes == 1 else (4, 2, 16, depth)
    return call(
        functools.partial(input_kernel, planes),
        [((4, count, PACKED), BF16), (part, F32), (part, F32)],
        [SMEM] + [VMEM] * 7,
        [],
        (16 * count * depth * (MAIN + TAIL), 4 * MAIN * depth),
        "input_products",
    )(at, weights[0], weights[1], tail, *pieces)


def weight_kernel(factor, x, g, *refs):
    chunks, (gate_out, up_out, down_out, turned) = refs[:-4], refs[-4:]

    @pl.when(pl.program_id(0) == 0)
    def _():
        first = 0
        for q in chunks:
            rows = q.shape[0]
            for start in range(0, PACKED, LANES):
                turned[start : start + LANES, first : first + rows] = q[:, start : start + LANES].T
            first += rows

    x_tail = dot(turned[3 * MAIN :], x[...], ((1,), (0,))) * factor
    g_tail = dot(turned[3 * MAIN :], g[...], ((1,), (0,))) * factor
    for i, (out, rows, tail) in enumerate(((down_out, g, g_tail), (gate_out, x, x_tail), (up_out, x, x_tail))):
        product = dot(turned[i * MAIN : (i + 1) * MAIN], rows[...], ((1,), (0,))) * factor
        out[:MAIN] = product.astype(BF16)
        out[MAIN:] = tail[i * STEP : i * STEP + TAIL].astype(BF16)


def weight_gradients(x, g, chunks, factor):
    tokens, depth = x.shape
    width = 512
    column = pl.BlockSpec((tokens, width), lambda i: (0, i))
    out = pl.BlockSpec((MAIN + TAIL, width), lambda i: (0, i))
    return pl.pallas_call(
        functools.partial(weight_kernel, factor),
        grid=(depth // width,),
        out_shape=[jax.ShapeDtypeStruct((MAIN + TAIL, depth), BF16)] * 3,
        in_specs=[column, column] + [pl.BlockSpec(q.shape, lambda i: (0, 0)) for q in chunks],
        out_specs=[out] * 3,
        scratch_shapes=[pltpu.VMEM((PACKED, tokens), BF16)],
        compiler_params=pltpu.CompilerParams(vmem_limit_bytes=40 * 2**20),
        cost_estimate=pl.CostEstimate(
            flops=6 * tokens * depth * (MAIN + TAIL), bytes_accessed=6 * MAIN * depth, transcendentals=0
        ),
        name="weight_products",
    )(x, g, *chunks)


def x_along(x, z, y, c, w):
    return (x + w, z, y, c)


def x_against(x, z, y, c, w):
    return (x - w, z, y, c)


def gather(tokens, out_grad):
    block = jnp.stack([tokens, out_grad])
    pair = jnp.stack([block, swap_cores(block)])
    line_across = send(block, lambda x, z, y, c, w: (x, z, y + 2, c))
    line_prev = send(pair, lambda x, z, y, c, w: (x, z, y + w, c))
    other = swap_cores(jnp.concatenate([line_prev, line_across[None]]))
    own = jnp.stack([pair, line_prev, other[1::-1], jnp.stack([line_across, other[2]])])
    prev = send(own, lambda x, z, y, c, w: (x, z + w, y, c))
    lines, cores = range(4), range(2)
    yield (own,), [(0, (l, c)) for l in lines for c in cores]
    last = yield prev
    half = after(own[:, 0], prev)
    following = swap_cores(prev)
    half = send(half, lambda x, z, y, c, w: (x, z + 2, y, c))
    last = yield (
        (prev, following),
        [b for l in lines for b in [(0, (l, 0)), (0, (l, 1)), (1, (FLIP[l], 1)), (1, (FLIP[l], 0))]],
    )
    other_half = swap_cores(after(half, last))
    yield (half, other_half), [b for l in lines for b in [(0, (l,)), (1, (FLIP[l],))]]


def local(tokens, out_grad, gate_weight, up_weight, down_weight):
    depth = tokens.shape[1]
    factor = 1.0 / math.sqrt(tokens.shape[0] * PLANES * LINES * CORES)
    me = lax.axis_index("row")
    way = 1 - 2 * lax.rem(lax.axis_index("col"), CORES)
    at = jnp.stack([lax.rem(me + off + 4, 4) for off in (0, -way, way, 2)])
    weights = (gate_weight.T, up_weight.T, down_weight)
    ends = [jnp.pad(w[MAIN:], ((0, STEP - TAIL), (0, 0))) for w in weights]
    none = jnp.zeros_like(ends[0])
    tails = (
        jnp.concatenate([ends[0], ends[1], none, none]),
        jnp.concatenate([none, none, ends[2], none]),
        jnp.concatenate([none, ends[0], ends[1], none]),
    )

    chunks = gather(tokens, out_grad)
    last = None
    state = [{} for _ in range(3)]

    for i, s in enumerate(state):
        sources, layout = chunks.send(last)
        if last is not None:
            sources = after(sources, last)
        s["x"], s["g"], far, near, relay, own = forward(at, weights, sources, layout)
        near = send(near, x_against)
        relay = (relay + send(far, x_along).astype(F32)).astype(BF16)
        if i == 0:
            prev = next(chunks)
            own = after(own, prev)
        mine = activation(own, near, send(relay, x_along))
        behind = send(mine, x_along)
        ahead = send(mine, x_against)
        pieces = (mine, behind, ahead, send(behind, x_along))
        q, keep, away = input_gradient(at, weights, tails[2], pieces)
        s["q"] = q.reshape(-1, PACKED)
        s["here"] = keep, swap_cores(away)
        if i == 0:
            last = mine
        else:
            last = far

    total = sum(state[0]["here"])
    here = sum(state[1]["here"])
    got = send(here.astype(BF16), lambda x, z, y, c, w: (x, z - w, y, c))
    here = sum(state[2]["here"])
    total += send(here.astype(BF16), lambda x, z, y, c, w: (x, z + 2, y, c)).astype(F32)
    all_x, all_g, all_q = ([s[k] for s in state] for k in ("x", "g", "q"))
    gate_wgrad, up_wgrad, down_wgrad = weight_gradients(
        after(jnp.concatenate(all_x), here), jnp.concatenate(all_g), all_q, factor
    )
    got = after(got, down_wgrad)
    rest = swap_cores(flip(got[:, 1]))
    total += got[:, 0].astype(F32) + rest.astype(F32)
    sent = total.astype(BF16)
    input_grad = (
        total[0]
        + send(sent[1], lambda x, z, y, c, w: (x, z, y - w, c)).astype(F32)
        + send(sent[2], lambda x, z, y, c, w: (x, z, y + w, c)).astype(F32)
        + send(sent[3], lambda x, z, y, c, w: (x, z, y + 2, c)).astype(F32)
    ).astype(BF16)
    return (input_grad, gate_wgrad.T, up_wgrad.T, down_wgrad)


def solution(mesh):
    placed = (P("col", "row"), P("col", "row"), P("row", "col"), P("row", "col"), P("col", "row"))
    return jax.shard_map(
        local,
        mesh=mesh,
        in_specs=placed,
        out_specs=(P("col", "row"), P("row", "col"), P("row", "col"), P("col", "row")),
        check_vma=False,
    )
```
